512 devices in a mesh: gx: 32 (over z, x_lo, core), gy: 16 (over x_hi, y).
Axes of the slice: x: 4 (x_hi: 2, x_lo: 2; x = x_hi * 2 + x_lo), y: 8, z: 8, core: 2. Of those that a mesh axis runs over, the one named last changes fastest.
Arguments:
- fields: float32 [2, 2, 16, 1024, 2048], P(None, None, None, 'gx', 'gy'), may hold values from -6 to 6
- wavenumber: float32 [16], P('gy'), may hold values from 0.5 to 2.5
- coupling: float32 [2, 16], P(None, 'gy'), may hold values from -3 to 3
- evanescent: int32 [16, 2048, 1024], P('gy', 'gx'), may hold values 0 or 1
Outputs:
- waves: float32 [2, 2, 16, 1024, 2048], P(None, None, None, 'gx', 'gy')
The draws below stay inside these ranges and needn't reach their ends.
All inputs are finite; a program needn't handle non-finite values. No bound on the sum of `evanescent` on one device may be relied on, other than what follows from the above.
Results may differ from the reference program's by a relative error of at most 0.000071.
Values sent between devices are 32-bit elements; how exact they have to be, the bound alone decides.
A program may use at most 64 MiB of HBM per device.

```python
import math
import jax
import jax.numpy as jnp
from jax import lax

NX = 1024
NY = 2048
FREQ = 16


def set_ends(drawn, rng, least, top_value):
    dims = drawn.shape
    spot = [jax.random.randint(jax.random.fold_in(rng, axis), (), 0, dims[axis]) for axis in range(len(dims))]
    drawn = drawn.at[tuple(spot)].set(least)
    longest = dims.index(max(dims))
    spot[longest] = (spot[longest] + 1) % dims[longest]
    return drawn.at[tuple(spot)].set(top_value)


def block_scale(rng, extent, shards, smallest, largest):
    def one(axis_at, parts):
        heights = jax.random.uniform(jax.random.fold_in(jax.random.fold_in(rng, 6), axis_at), (parts,), jnp.float32, smallest / len(shards), largest / len(shards))
        return jnp.repeat(jnp.exp(heights), extent[axis_at] // parts).reshape((-1,) + (1,) * (len(extent) - axis_at - 1))

    gain = one(*shards[0])
    for cut in shards[1:]:
        gain = gain * one(*cut)
    return gain


def noise(own_key, dims, width, reach, shards=(), kind=jnp.bfloat16):
    entries = width * jax.random.normal(own_key, dims, jnp.float32)
    if shards:
        entries = entries * block_scale(own_key, dims, shards, -0.22, 0.18)
    return jnp.clip(entries, -reach, reach).astype(kind)


def setup_inputs(seed: int = 0) -> dict:
    key_of = jax.random.split(jax.random.key(seed), 5)
    fields = noise(key_of[0], (2, 2, FREQ, NX, NY), 1.0, 6.0, ((3, 32), (4, 16)), jnp.float32)
    wavenumber = jnp.clip(jnp.exp(math.log(2.5) - 1.609438 * jax.random.uniform(key_of[1], (FREQ,), jnp.float32) ** block_scale(key_of[1], (FREQ,), ((0, 16),), -0.2, 0.2)), 0.5, 2.5)
    coupling = noise(key_of[2], (2, FREQ), 1.0, 3.0, ((1, 16),), jnp.float32)
    evanescent = set_ends((jax.random.randint(key_of[3], (FREQ, NY, NX), 0, 4) < 1).astype(jnp.int32), jax.random.fold_in(key_of[3], 1), 0, 1)
    return {"fields": fields, "wavenumber": wavenumber, "coupling": coupling, "evanescent": evanescent}


def compose_slice(inputs):
    block, radius, coef, muted = inputs
    pressure = block[0, 0] + 1j * block[0, 1]
    velocity = block[1, 0] + 1j * block[1, 1]
    spec_press = jnp.fft.fft2(pressure)
    spec_vel = jnp.fft.fft2(velocity)
    kx_wave = 2.0 * jnp.pi * jnp.fft.fftfreq(NX)
    ky_wave = 2.0 * jnp.pi * jnp.fft.fftfreq(NY)
    squared = radius * radius - kx_wave[:, None] ** 2 - ky_wave[None, :] ** 2
    open_mask = (1 - muted.T).astype(squared.dtype)
    vertical = jnp.sqrt(jnp.maximum(squared, 0.0)) * open_mask
    factor = vertical * (coef[0] + 1j * coef[1])
    upward = 0.5 * (spec_press - factor * spec_vel)
    downward = 0.5 * (spec_press + factor * spec_vel)
    up_space = jnp.fft.ifft2(upward)
    down_space = jnp.fft.ifft2(downward)
    return jnp.stack([jnp.stack([up_space.real, up_space.imag]), jnp.stack([down_space.real, down_space.imag])]).astype(block.dtype)

def reference(fields, wavenumber, coupling, evanescent):
    slices = lax.map(compose_slice, (jnp.moveaxis(fields, 2, 0), wavenumber, coupling.T, evanescent))
    return jnp.moveaxis(slices, 0, 2)
```

```python
import functools
import math

import jax
import jax.numpy as jnp
import ml_dtypes
import numpy as np
from jax import lax
from jax.experimental import pallas as pl
from jax.experimental.pallas import tpu as pltpu
from jax.sharding import PartitionSpec as P

MESH = pl.DeviceIdType.MESH
NX, NY = 1024, 2048
GX, GY = 32, 16
CH = 4
NT = (((1,), (1,)), ((), ()))
NN = (((1,), (0,)), ((), ()))


def halves(table):
    high = table.astype(ml_dtypes.bfloat16)
    low = (table - high.astype(np.float64)).astype(ml_dtypes.bfloat16)
    return [high, low]


def real_form(angle):
    cos, sin = np.cos(angle), np.sin(angle)
    return np.array([[cos, sin], [-sin, cos]])


def tables():
    form = real_form(2 * np.pi * (np.arange(128)[:, None] * np.arange(128)[None, :] % 128) / 128)
    wave_y = form.reshape(2, 2, 32, 4, 128).transpose(2, 0, 3, 1, 4).reshape(256, 256)
    form = real_form(2 * np.pi * (np.arange(32)[:, None] * np.arange(32)[None, :] % 32) / 32)
    wave_i = np.einsum("qpim,kl->ipkqlm", form, np.eye(4)).reshape(256, 256)
    wave_r = np.einsum("qpmcr,kl->qmkpclr", form.reshape(2, 2, 32, 4, 8), np.eye(8)).reshape(512, 512)
    small = np.stack(halves(wave_y) + halves(wave_i))
    back = wave_r.T.reshape(2, 4, 64, 512).transpose(1, 0, 2, 3).reshape(512, 512)
    large = np.stack(halves(wave_r) + halves(back))
    turn_y = 2 * np.pi * np.arange(16)[:, None] * np.arange(128)[None, :] / NY
    turn_x = 2 * np.pi * np.arange(32)[:, None] * np.tile(np.arange(32), 4)[None, :] / NX
    turns = np.concatenate([np.cos(turn_y), np.sin(turn_y), np.cos(turn_x), np.sin(turn_x)])
    return small, large, turns.astype(np.float32)


def split(value):
    high = value.astype(jnp.bfloat16)
    low = (value - high.astype(jnp.float32)).astype(jnp.bfloat16)
    return high, low


def product(left, right, dims):
    def dot(a, b):
        return lax.dot_general(a, b, dims, preferred_element_type=jnp.float32)

    return dot(left[0], right[0]) + (dot(left[0], right[1]) + dot(left[1], right[0]))


def times(value, cos, sin, orient):
    real, imag = value
    if orient < 0:
        return real * cos + imag * sin, imag * cos - real * sin
    return real * cos - imag * sin, imag * cos + real * sin


def add(a, b):
    return a[0] + b[0], a[1] + b[1]


def sub(a, b):
    return a[0] - b[0], a[1] - b[1]


def quarter(a, orient):
    return (a[1], -a[0]) if orient < 0 else (-a[1], a[0])


def constant_turn(value, step, orient):
    step %= 16
    if step == 0:
        return value
    if step == 4:
        return quarter(value, orient)
    angle = 2 * math.pi * step / 16
    return times(value, math.cos(angle), math.sin(angle), orient)


def four(v, orient):
    a, b = add(v[0], v[2]), sub(v[0], v[2])
    c, d = add(v[1], v[3]), quarter(sub(v[1], v[3]), orient)
    return [add(a, c), add(b, d), sub(a, c), sub(b, d)]


def sixteen(v, orient):
    inner = [four([v[n + 4 * m] for m in range(4)], orient) for n in range(4)]
    out = [None] * 16
    for k in range(4):
        for m, value in enumerate(four([constant_turn(inner[n][k], n * k, orient) for n in range(4)], orient)):
            out[k + 4 * m] = value
    return out


def forward_y(values, turn_cos, turn_sin, table):
    spec = sixteen(values, -1)
    spec = [times(spec[k], turn_cos(k), turn_sin(k), -1) for k in range(16)]
    real = jnp.concatenate([s[0] for s in spec], axis=0)
    imag = jnp.concatenate([s[1] for s in spec], axis=0)
    return product(table, split(jnp.concatenate([real, imag], axis=1)), NT)


def inverse_y(block, turn_cos, turn_sin, table):
    spec = product(split(block.T), table, NN)
    spec = [(spec[8 * k : 8 * k + 8, :128], spec[8 * k : 8 * k + 8, 128:]) for k in range(16)]
    return sixteen([times(spec[k], turn_cos(k), turn_sin(k), 1) for k in range(16)], 1)


def forward_x(block, cos, sin, table):
    spec = product(split(block.T), table, NN)
    value = (spec[:, :128].reshape(16, 8, 128), spec[:, 128:].reshape(16, 8, 128))
    parts = times(value, cos[None], sin[None], -1)
    parts = [part.reshape(128, 128) for part in parts]
    return [jnp.concatenate([part[:64], part[64:]], axis=1) for part in parts]


def inverse_x(value, cos, sin, table):
    parts = [jnp.concatenate([p[:, :128], p[:, 128:]], axis=0).reshape(16, 8, 128) for p in (value[:64], value[64:])]
    parts = times(parts, cos[None], sin[None], 1)
    return product(table, split(jnp.concatenate([p.reshape(128, 128) for p in parts], axis=1)), NT)


def kernel(
    fields, radius, coef, muted, small_in, large_in, turns_in, out,
    small, large, turns, mask, vert, ybuf, xsrc, xbuf, ehigh, elow, vsrc, vbuf, wsrc, local, send, recv,
):
    gx, gy = lax.axis_index("gx"), lax.axis_index("gy")

    loads = [
        pltpu.make_async_copy(muted.at[0], mask, local.at[0]),
        pltpu.make_async_copy(turns_in, turns, local.at[1]),
        pltpu.make_async_copy(small_in, small, local.at[2]),
        pltpu.make_async_copy(large_in, large, local.at[3]),
    ]
    rows = [pl.ds(8 * c, 8) for c in range(CH)]
    own = [pltpu.make_async_copy(fields.at[1, :, gy, rows[c]], ybuf.at[c, gy], local.at[4 + c]) for c in range(CH)]
    for copy in loads + own:
        copy.start()

    barrier = pltpu.get_barrier_semaphore()

    def greet_y(k, carry):
        pl.semaphore_signal(barrier, inc=1, device_id=(gx, lax.rem(gy + k, GY)), device_id_type=MESH)
        return carry

    def greet_x(k, carry):
        pl.semaphore_signal(barrier, inc=1, device_id=(lax.rem(gx + k, GX), gy), device_id_type=MESH)
        return carry

    lax.fori_loop(1, GY, greet_y, 0)
    lax.fori_loop(1, GX, greet_x, 0)
    pl.semaphore_wait(barrier, GX + GY - 2)

    def over_y(phase, c, source, target):
        def one(k, carry):
            peer = lax.rem(gy + k, GY)
            pltpu.make_async_remote_copy(
                src_ref=source(peer), dst_ref=target, send_sem=send.at[phase, c], recv_sem=recv.at[phase, c],
                device_id=(gx, peer), device_id_type=MESH,
            ).start()
            return carry

        lax.fori_loop(1, GY, one, 0)

    def over_x(phase, c, source, target):
        def one(k, carry):
            peer = lax.rem(gx + k, GX)
            pltpu.make_async_remote_copy(
                src_ref=source(peer), dst_ref=target, send_sem=send.at[phase, c], recv_sem=recv.at[phase, c],
                device_id=(peer, gy), device_id_type=MESH,
            ).start()
            return carry

        lax.fori_loop(1, GX, one, 0)

    def wait(buffer, semaphore):
        pltpu.make_async_copy(buffer, buffer, semaphore).wait()

    for c in range(CH):
        over_y(0, c, lambda peer, c=c: fields.at[1, :, peer, rows[c]], ybuf.at[c, gy])

    loads[0].wait()
    lane = lax.broadcasted_iota(jnp.int32, (16, 128), 1)
    row = lax.broadcasted_iota(jnp.int32, (16, 128), 0)
    ky = 64 * gx + 16 * (lane // 32) + row
    ky_wave = (2.0 * math.pi / NY) * jnp.where(ky < NY // 2, ky, ky - NY).astype(jnp.float32)
    square = radius[0] * radius[0]

    def factor(g, carry):
        columns = pl.ds(pl.multiple_of(128 * g, 128), 128)
        for m in range(4):
            picked = None
            for k in range(4):
                piece = mask[16 * k : 16 * k + 16, columns]
                if k != m:
                    piece = pltpu.roll(piece, 32 * (k - m) % 128, 1)
                picked = piece if picked is None else jnp.where(lane // 32 == k, piece, picked)
            kx = lane % 32 + 32 * (4 * g + m)
            kx_wave = (2.0 * math.pi / NX) * jnp.where(kx < NX // 2, kx, kx - NX).astype(jnp.float32)
            depth = jnp.sqrt(jnp.maximum(square - kx_wave * kx_wave - ky_wave * ky_wave, 0.0))
            depth = depth * (1 - picked).astype(jnp.float32)
            place = pl.ds(pl.multiple_of(32 * g + 8 * m, 8), 8)
            vert[place, 0:128] = depth[0:8]
            vert[place, 128:256] = depth[8:16]
        return carry

    lax.fori_loop(0, 8, factor, 0)
    for load in loads[1:]:
        load.wait()

    table_y = (small[0], small[1])
    table_i = (small[2], small[3])

    def turn_y(part):
        return lambda k: turns[16 * part + k : 16 * part + k + 1, :]

    def turn_x(c):
        return turns[pl.ds(32 + 8 * c, 8), :], turns[pl.ds(64 + 8 * c, 8), :]

    for c in range(CH):
        own[c].wait()
        wait(ybuf.at[c, pl.ds(0, GY - 1)], recv.at[0, c])
        values = [(ybuf[c, j, 0], ybuf[c, j, 1]) for j in range(GY)]
        xsrc[c] = forward_y(values, turn_y(0), turn_y(1), table_y).reshape(GX, 8, 128)
        over_x(1, c, lambda peer, c=c: xsrc.at[c, peer], xbuf.at[c, gx])
        xbuf[c, gx] = xsrc[c, gx]

    for c in range(CH):
        wait(xbuf.at[c, pl.ds(0, GX - 1)], recv.at[1, c])
        parts = forward_x(xbuf[c].reshape(256, 128), *turn_x(c), table_i)
        for part in range(2):
            high, low = split(parts[part])
            ehigh[256 * part + 64 * c : 256 * part + 64 * c + 64, :] = high
            elow[256 * part + 64 * c : 256 * part + 64 * c + 64, :] = low

    spec = product((large[0], large[1]), (ehigh[...], elow[...]), NN)
    scale = 0.5 / (NX * NY)
    coef_real, coef_imag = coef[0, 0] * scale, coef[1, 0] * scale
    real, imag = spec[:256], spec[256:]
    depth = vert[...]
    real, imag = (
        depth * coef_real * real - depth * coef_imag * imag,
        depth * coef_real * imag + depth * coef_imag * real,
    )
    high, low = split(jnp.concatenate([real, imag], axis=0))

    for c in range(CH):
        back = (large[2, 128 * c : 128 * c + 128, :], large[3, 128 * c : 128 * c + 128, :])
        value = product(back, (high, low), NN)
        vsrc[c] = inverse_x(value, *turn_x(c), table_i).reshape(GX, 8, 128)
        over_x(2, c, lambda peer, c=c: vsrc.at[c, peer], vbuf.at[c, gx])
        vbuf[c, gx] = vsrc[c, gx]

    for c in range(CH):
        wait(vbuf.at[c, pl.ds(0, GX - 1)], recv.at[2, c])
        values = inverse_y(vbuf[c].reshape(256, 128), turn_y(0), turn_y(1), table_y)
        for j in range(GY):
            wsrc[c, j, 0] = values[j][0]
            wsrc[c, j, 1] = values[j][1]
        over_y(3, c, lambda peer, c=c: wsrc.at[c, peer], out.at[:, gy, rows[c]])
        pltpu.make_async_copy(wsrc.at[c, gy], out.at[:, gy, rows[c]], local.at[8 + c]).start()

    for c in range(CH):
        pltpu.make_async_copy(wsrc.at[c, gy], out.at[:, gy, rows[c]], local.at[8 + c]).wait()
        wait(ybuf.at[c, pl.ds(0, GY - 1)], recv.at[3, c])
        wait(ybuf.at[c, pl.ds(0, GY - 1)], send.at[0, c])
        wait(xbuf.at[c, pl.ds(0, GX - 1)], send.at[1, c])
        wait(vbuf.at[c, pl.ds(0, GX - 1)], send.at[2, c])
        wait(ybuf.at[c, pl.ds(0, GY - 1)], send.at[3, c])


def shards(fields, wavenumber, coupling, evanescent):
    small, large, turns = tables()
    anywhere = pl.BlockSpec(memory_space=pl.ANY)
    scalars = pl.BlockSpec(memory_space=pltpu.SMEM)
    wave = pl.pallas_call(
        kernel,
        out_shape=jax.ShapeDtypeStruct((2, GY, 32, 128), jnp.float32),
        in_specs=[anywhere, scalars, scalars, anywhere, anywhere, anywhere, anywhere],
        out_specs=anywhere,
        scratch_shapes=[
            pltpu.VMEM((4, 256, 256), jnp.bfloat16),
            pltpu.VMEM((4, 512, 512), jnp.bfloat16),
            pltpu.VMEM((96, 128), jnp.float32),
            pltpu.VMEM((64, 1024), jnp.int32),
            pltpu.VMEM((256, 256), jnp.float32),
            pltpu.VMEM((CH, GY, 2, 8, 128), jnp.float32),
            pltpu.VMEM((CH, GX, 8, 128), jnp.float32),
            pltpu.VMEM((CH, GX, 8, 128), jnp.float32),
            pltpu.VMEM((512, 256), jnp.bfloat16),
            pltpu.VMEM((512, 256), jnp.bfloat16),
            pltpu.VMEM((CH, GX, 8, 128), jnp.float32),
            pltpu.VMEM((CH, GX, 8, 128), jnp.float32),
            pltpu.VMEM((CH, GY, 2, 8, 128), jnp.float32),
            pltpu.SemaphoreType.DMA((12,)),
            pltpu.SemaphoreType.DMA((4, CH)),
            pltpu.SemaphoreType.DMA((4, CH)),
        ],
        compiler_params=pltpu.CompilerParams(
            collective_id=0, has_side_effects=True, vmem_limit_bytes=48 * 1024 * 1024
        ),
    )(fields, wavenumber, coupling, evanescent, jnp.asarray(small), jnp.asarray(large), jnp.asarray(turns))
    press = 0.5 * fields[0]
    return jnp.stack([press - wave, press + wave])


def solution(mesh):
    in_specs = (P(None, None, None, "gx", "gy"), P("gy"), P(None, "gy"), P("gy", "gx", None))
    out_specs = P(None, None, None, "gx", "gy")
    return jax.shard_map(shards, mesh=mesh, in_specs=in_specs, out_specs=out_specs, check_vma=False)
```

```python
import functools
import math

import jax
import jax.numpy as jnp
import ml_dtypes
import numpy as np
from jax import lax
from jax.experimental import pallas as pl
from jax.experimental.pallas import tpu as pltpu
from jax.sharding import PartitionSpec as P

MESH = pl.DeviceIdType.MESH
NX, NY = 1024, 2048
GX, GY = 32, 16
CH = 4
AHEAD = 4
TOP = int(2.5 * NY / (2 * math.pi))
IDLE_FROM, IDLE_TO = TOP // 64 + 1, (NY - TOP) // 64
BUSY = GX - (IDLE_TO - IDLE_FROM)
NT = (((1,), (1,)), ((), ()))
NN = (((1,), (0,)), ((), ()))


def halves(table):
    high = table.astype(ml_dtypes.bfloat16)
    low = (table - high.astype(np.float64)).astype(ml_dtypes.bfloat16)
    return [high, low]


def real_form(angle):
    cos, sin = np.cos(angle), np.sin(angle)
    return np.array([[cos, sin], [-sin, cos]])


def tables():
    form = real_form(2 * np.pi * (np.arange(128)[:, None] * np.arange(128)[None, :] % 128) / 128)
    wave_y = form.reshape(2, 2, 32, 4, 128).transpose(2, 0, 3, 1, 4).reshape(256, 256)
    form = real_form(2 * np.pi * (np.arange(32)[:, None] * np.arange(32)[None, :] % 32) / 32)
    wave_i = np.einsum("qpim,kl->ipkqlm", form, np.eye(4)).reshape(256, 256)
    wave_r = np.einsum("qpmcr,kl->qmkpclr", form.reshape(2, 2, 32, 4, 8), np.eye(8)).reshape(512, 512)
    small = np.stack(halves(wave_y) + halves(wave_i))
    back = wave_r.T.reshape(2, 4, 64, 512).transpose(1, 0, 2, 3).reshape(512, 512)
    large = np.stack(halves(wave_r) + halves(back))
    turn_y = 2 * np.pi * np.arange(16)[:, None] * np.arange(128)[None, :] / NY
    turn_x = 2 * np.pi * np.arange(32)[:, None] * np.tile(np.arange(32), 4)[None, :] / NX
    turns = np.concatenate([np.cos(turn_y), np.sin(turn_y), np.cos(turn_x), np.sin(turn_x)])
    return small, large, turns.astype(np.float32)


def split(value):
    high = value.astype(jnp.bfloat16)
    low = (value - high.astype(jnp.float32)).astype(jnp.bfloat16)
    return high, low


def product(left, right, dims):
    def dot(a, b):
        return lax.dot_general(a, b, dims, preferred_element_type=jnp.float32)

    return dot(left[0], right[0]) + (dot(left[0], right[1]) + dot(left[1], right[0]))


def times(value, cos, sin, orient):
    real, imag = value
    if orient < 0:
        return real * cos + imag * sin, imag * cos - real * sin
    return real * cos - imag * sin, imag * cos + real * sin


def add(a, b):
    return a[0] + b[0], a[1] + b[1]


def sub(a, b):
    return a[0] - b[0], a[1] - b[1]


def quarter(a, orient):
    return (a[1], -a[0]) if orient < 0 else (-a[1], a[0])


def constant_turn(value, step, orient):
    step %= 16
    if step == 0:
        return value
    if step == 4:
        return quarter(value, orient)
    angle = 2 * math.pi * step / 16
    return times(value, math.cos(angle), math.sin(angle), orient)


def four(v, orient):
    a, b = add(v[0], v[2]), sub(v[0], v[2])
    c, d = add(v[1], v[3]), quarter(sub(v[1], v[3]), orient)
    return [add(a, c), add(b, d), sub(a, c), sub(b, d)]


def sixteen(v, orient):
    inner = [four([v[n + 4 * m] for m in range(4)], orient) for n in range(4)]
    out = [None] * 16
    for k in range(4):
        for m, value in enumerate(four([constant_turn(inner[n][k], n * k, orient) for n in range(4)], orient)):
            out[k + 4 * m] = value
    return out


def forward_y(values, turn_cos, turn_sin, table):
    spec = sixteen(values, -1)
    spec = [times(spec[k], turn_cos(k), turn_sin(k), -1) for k in range(16)]
    real = jnp.concatenate([s[0] for s in spec], axis=0)
    imag = jnp.concatenate([s[1] for s in spec], axis=0)
    return product(table, split(jnp.concatenate([real, imag], axis=1)), NT)


def inverse_y(block, turn_cos, turn_sin, table):
    spec = product(split(block.T), table, NN)
    spec = [(spec[8 * k : 8 * k + 8, :128], spec[8 * k : 8 * k + 8, 128:]) for k in range(16)]
    return sixteen([times(spec[k], turn_cos(k), turn_sin(k), 1) for k in range(16)], 1)


def forward_x(block, cos, sin, table):
    spec = product(split(block.T), table, NN)
    value = (spec[:, :128].reshape(16, 8, 128), spec[:, 128:].reshape(16, 8, 128))
    parts = times(value, cos[None], sin[None], -1)
    parts = [part.reshape(128, 128) for part in parts]
    return [jnp.concatenate([part[:64], part[64:]], axis=1) for part in parts]


def inverse_x(value, cos, sin, table):
    parts = [jnp.concatenate([p[:, :128], p[:, 128:]], axis=0).reshape(16, 8, 128) for p in (value[:64], value[64:])]
    parts = times(parts, cos[None], sin[None], 1)
    return product(table, split(jnp.concatenate([p.reshape(128, 128) for p in parts], axis=1)), NT)


def kernel(
    fields, radius, coef, muted, small_in, large_in, turns_in, out,
    small, large, turns, mask, vert, vel, ybuf, xsrc, xbuf, ehigh, elow, vsrc, vbuf, wsrc, local, send, recv,
):
    gx, gy = lax.axis_index("gx"), lax.axis_index("gy")
    busy = jnp.logical_or(gx < IDLE_FROM, gx >= IDLE_TO)
    idle = jnp.logical_not(busy)
    barrier = pltpu.get_barrier_semaphore()

    load_vel = pltpu.make_async_copy(fields.at[1], vel, local.at[4])
    load_vel.start()

    def peer_y(k):
        turn = (k - 1) // 2
        far = 4 - (turn + 1) // 2
        y = lax.rem(gy + 8 + jnp.where(lax.rem(turn, 2) == 1, far, -far), 8)
        return 8 * lax.rem(gy // 8 + k, 2) + y

    def peer_x(k):
        turn = k // 4
        far = 4 - (turn + 1) // 2
        z = lax.rem(gx // 4 + 8 + jnp.where(lax.rem(turn, 2) == 1, far, -far), 8)
        return 4 * z + lax.rem(gx + 3 - lax.rem(k, 4), 4)

    def greet_y(k, carry):
        pl.semaphore_signal(barrier, inc=1, device_id=(gx, peer_y(k)), device_id_type=MESH)
        return carry

    def greet_x(k, carry):
        pl.semaphore_signal(barrier, inc=1, device_id=(peer_x(k), gy), device_id_type=MESH)
        return carry

    lax.fori_loop(0, GX - 1, greet_x, 0)
    lax.fori_loop(1, GY, greet_y, 0)

    loads = [
        pltpu.make_async_copy(muted.at[0], mask, local.at[0]),
        pltpu.make_async_copy(turns_in, turns, local.at[1]),
        pltpu.make_async_copy(small_in, small, local.at[2]),
        pltpu.make_async_copy(large_in, large, local.at[3]),
    ]
    rows = [pl.ds(8 * c, 8) for c in range(CH)]

    def over_y(phase, c, source, target):
        def one(k, carry):
            peer = peer_y(k)
            pltpu.make_async_remote_copy(
                src_ref=source(peer), dst_ref=target, send_sem=send.at[phase, c], recv_sem=recv.at[phase, c],
                device_id=(gx, peer), device_id_type=MESH,
            ).start()
            return carry

        lax.fori_loop(1, GY, one, 0)

    def over_x(phase, c, source, target, busy_only):
        def one(k, carry):
            peer = peer_x(k)

            def go():
                pltpu.make_async_remote_copy(
                    src_ref=source(peer), dst_ref=target, send_sem=send.at[phase, c], recv_sem=recv.at[phase, c],
                    device_id=(peer, gy), device_id_type=MESH,
                ).start()

            if busy_only:
                pl.when(jnp.logical_or(peer < IDLE_FROM, peer >= IDLE_TO))(go)
            else:
                go()
            return carry

        lax.fori_loop(0, GX - 1, one, 0)

    def wait(buffer, semaphore):
        pltpu.make_async_copy(buffer, buffer, semaphore).wait()

    def first_y(c):
        over_y(0, c, lambda peer: vel.at[:, peer, rows[c]], ybuf.at[c, gy])

    load_vel.wait()
    pl.semaphore_wait(barrier, GX + GY - 2)
    for c in range(AHEAD):
        first_y(c)
    for load in loads:
        load.start()

    lane = lax.broadcasted_iota(jnp.int32, (16, 128), 1)
    row = lax.broadcasted_iota(jnp.int32, (16, 128), 0)
    ky = 64 * gx + 16 * (lane // 32) + row
    ky_wave = (2.0 * math.pi / NY) * jnp.where(ky < NY // 2, ky, ky - NY).astype(jnp.float32)
    square = radius[0] * radius[0]

    def factor(g, carry):
        columns = pl.ds(pl.multiple_of(128 * g, 128), 128)
        for m in range(4):
            picked = None
            for k in range(4):
                piece = mask[16 * k : 16 * k + 16, columns]
                if k != m:
                    piece = pltpu.roll(piece, 32 * (k - m) % 128, 1)
                picked = piece if picked is None else jnp.where(lane // 32 == k, piece, picked)
            kx = lane % 32 + 32 * (4 * g + m)
            kx_wave = (2.0 * math.pi / NX) * jnp.where(kx < NX // 2, kx, kx - NX).astype(jnp.float32)
            depth = jnp.sqrt(jnp.maximum(square - kx_wave * kx_wave - ky_wave * ky_wave, 0.0))
            depth = depth * (1 - picked).astype(jnp.float32)
            place = pl.ds(pl.multiple_of(32 * g + 8 * m, 8), 8)
            vert[place, 0:128] = depth[0:8]
            vert[place, 128:256] = depth[8:16]
        return carry

    for c in range(CH):
        ybuf[c, gy] = vel[:, gy, rows[c]]
        vbuf[c, IDLE_FROM:IDLE_TO] = jnp.zeros((IDLE_TO - IDLE_FROM, 8, 128), jnp.float32)
    for load in loads:
        load.wait()
    lax.fori_loop(0, 8, factor, 0)

    table_y = (small[0], small[1])
    table_i = (small[2], small[3])

    def turn_y(part):
        return lambda k: turns[16 * part + k : 16 * part + k + 1, :]

    def turn_x(c):
        return turns[pl.ds(32 + 8 * c, 8), :], turns[pl.ds(64 + 8 * c, 8), :]

    for c in range(CH):
        wait(ybuf.at[c, pl.ds(0, GY - 1)], recv.at[0, c])
        if c + AHEAD < CH:
            first_y(c + AHEAD)
        values = [(ybuf[c, j, 0], ybuf[c, j, 1]) for j in range(GY)]
        xsrc[c] = forward_y(values, turn_y(0), turn_y(1), table_y).reshape(GX, 8, 128)
        over_x(1, c, lambda peer: xsrc.at[c, peer], xbuf.at[c, gx], True)
        xbuf[c, gx] = xsrc[c, gx]

    @pl.when(busy)
    def spectrum():
        for c in range(CH):
            wait(xbuf.at[c, pl.ds(0, GX - 1)], recv.at[1, c])
            parts = forward_x(xbuf[c].reshape(256, 128), *turn_x(c), table_i)
            for part in range(2):
                high, low = split(parts[part])
                ehigh[256 * part + 64 * c : 256 * part + 64 * c + 64, :] = high
                elow[256 * part + 64 * c : 256 * part + 64 * c + 64, :] = low

        spec = product((large[0], large[1]), (ehigh[...], elow[...]), NN)
        scale = 0.5 / (NX * NY)
        coef_real, coef_imag = coef[0] * scale, coef[1] * scale
        real, imag = spec[:256], spec[256:]
        depth = vert[...]
        real, imag = (
            depth * coef_real * real - depth * coef_imag * imag,
            depth * coef_real * imag + depth * coef_imag * real,
        )
        high, low = split(jnp.concatenate([real, imag], axis=0))

        for c in range(CH):
            back = (large[2, 128 * c : 128 * c + 128, :], large[3, 128 * c : 128 * c + 128, :])
            value = product(back, (high, low), NN)
            vsrc[c] = inverse_x(value, *turn_x(c), table_i).reshape(GX, 8, 128)
            over_x(2, c, lambda peer: vsrc.at[c, peer], vbuf.at[c, gx], False)
            vbuf[c, gx] = vsrc[c, gx]

    for c in range(CH):
        pl.when(busy)(lambda: wait(vbuf.at[c, pl.ds(0, BUSY - 1)], recv.at[2, c]))
        pl.when(idle)(lambda: wait(vbuf.at[c, pl.ds(0, BUSY)], recv.at[2, c]))
        values = inverse_y(vbuf[c].reshape(256, 128), turn_y(0), turn_y(1), table_y)
        for j in range(GY):
            wsrc[c, j, 0] = values[j][0]
            wsrc[c, j, 1] = values[j][1]
        over_y(3, c, lambda peer: wsrc.at[c, peer], out.at[:, gy, rows[c]])
        pltpu.make_async_copy(wsrc.at[c, gy], out.at[:, gy, rows[c]], local.at[5 + c]).start()

    for c in range(CH):
        wait(ybuf.at[c, pl.ds(0, GY - 1)], send.at[0, c])
        pl.when(busy)(lambda: wait(xbuf.at[c, pl.ds(0, BUSY - 1)], send.at[1, c]))
        pl.when(idle)(lambda: wait(xbuf.at[c, pl.ds(0, BUSY)], send.at[1, c]))
        pl.when(busy)(lambda: wait(vbuf.at[c, pl.ds(0, GX - 1)], send.at[2, c]))
        pltpu.make_async_copy(wsrc.at[c, gy], out.at[:, gy, rows[c]], local.at[5 + c]).wait()
        wait(ybuf.at[c, pl.ds(0, GY - 1)], send.at[3, c])
        wait(ybuf.at[c, pl.ds(0, GY - 1)], recv.at[3, c])


def shards(fields, wavenumber, coupling, evanescent):
    small, large, turns = tables()
    hbm = pl.BlockSpec(memory_space=pltpu.HBM)
    scalars = pl.BlockSpec(memory_space=pltpu.SMEM)
    wave = pl.pallas_call(
        kernel,
        out_shape=pltpu.VMEM((2, GY, 32, 128), jnp.float32),
        in_specs=[hbm, scalars, scalars, hbm, hbm, hbm, hbm],
        out_specs=pl.BlockSpec(memory_space=pl.ANY),
        scratch_shapes=[
            pltpu.VMEM((4, 256, 256), jnp.bfloat16),
            pltpu.VMEM((4, 512, 512), jnp.bfloat16),
            pltpu.VMEM((96, 128), jnp.float32),
            pltpu.VMEM((64, 1024), jnp.int32),
            pltpu.VMEM((256, 256), jnp.float32),
            pltpu.VMEM((2, GY, 32, 128), jnp.float32),
            pltpu.VMEM((CH, GY, 2, 8, 128), jnp.float32),
            pltpu.VMEM((CH, GX, 8, 128), jnp.float32),
            pltpu.VMEM((CH, GX, 8, 128), jnp.float32),
            pltpu.VMEM((512, 256), jnp.bfloat16),
            pltpu.VMEM((512, 256), jnp.bfloat16),
            pltpu.VMEM((CH, GX, 8, 128), jnp.float32),
            pltpu.VMEM((CH, GX, 8, 128), jnp.float32),
            pltpu.VMEM((CH, GY, 2, 8, 128), jnp.float32),
            pltpu.SemaphoreType.DMA((12,)),
            pltpu.SemaphoreType.DMA((4, CH)),
            pltpu.SemaphoreType.DMA((4, CH)),
        ],
        compiler_params=pltpu.CompilerParams(
            collective_id=0, has_side_effects=True, vmem_limit_bytes=60 * 1024 * 1024
        ),
    )(fields, wavenumber, coupling.reshape(2), evanescent, jnp.asarray(small), jnp.asarray(large), jnp.asarray(turns))
    press = 0.5 * fields[0]
    return jnp.stack([press - wave, press + wave])


def solution(mesh):
    in_specs = (P(None, None, None, "gx", "gy"), P("gy"), P(None, "gy"), P("gy", "gx", None))
    out_specs = P(None, None, None, "gx", "gy")
    return jax.shard_map(shards, mesh=mesh, in_specs=in_specs, out_specs=out_specs, check_vma=False)
```

```python
import functools
import math

import jax
import jax.numpy as jnp
import ml_dtypes
import numpy as np
from jax import lax
from jax.experimental import pallas as pl
from jax.experimental.pallas import tpu as pltpu
from jax.sharding import PartitionSpec as P

MESH = pl.DeviceIdType.MESH
NX, NY = 1024, 2048
GX, GY = 32, 16
CH = 4
AHEAD = 4
TOP = int(2.5 * NY / (2 * math.pi))
IDLE_FROM, IDLE_TO = TOP // 64 + 1, (NY - TOP) // 64
BUSY = GX - (IDLE_TO - IDLE_FROM)
NT = (((1,), (1,)), ((), ()))
NN = (((1,), (0,)), ((), ()))


def halves(table):
    high = table.astype(ml_dtypes.bfloat16)
    low = (table - high.astype(np.float64)).astype(ml_dtypes.bfloat16)
    return [high, low]


def real_form(angle):
    cos, sin = np.cos(angle), np.sin(angle)
    return np.array([[cos, sin], [-sin, cos]])


def tables():
    form = real_form(2 * np.pi * (np.arange(128)[:, None] * np.arange(128)[None, :] % 128) / 128)
    wave_y = form.reshape(2, 2, 32, 4, 128).transpose(2, 0, 3, 1, 4).reshape(256, 256)
    form = real_form(2 * np.pi * (np.arange(32)[:, None] * np.arange(32)[None, :] % 32) / 32)
    wave_i = np.einsum("qpim,kl->ipkqlm", form, np.eye(4)).reshape(256, 256)
    wave_r = np.einsum("qpmcr,kl->qmkpclr", form.reshape(2, 2, 32, 4, 8), np.eye(8)).reshape(512, 512)
    small = np.stack(halves(wave_y) + halves(wave_i))
    back = wave_r.T.reshape(2, 4, 64, 512).transpose(1, 0, 2, 3).reshape(512, 512)
    large = np.stack(halves(wave_r) + halves(back))
    turn_y = 2 * np.pi * np.arange(16)[:, None] * np.arange(128)[None, :] / NY
    turn_x = 2 * np.pi * np.arange(32)[:, None] * np.tile(np.arange(32), 4)[None, :] / NX
    turns = np.concatenate([np.cos(turn_y), np.sin(turn_y), np.cos(turn_x), np.sin(turn_x)])
    return small, large, turns.astype(np.float32)


def split(value):
    high = value.astype(jnp.bfloat16)
    low = (value - high.astype(jnp.float32)).astype(jnp.bfloat16)
    return high, low


def product(left, right, dims):
    def dot(a, b):
        return lax.dot_general(a, b, dims, preferred_element_type=jnp.float32)

    return dot(left[0], right[0]) + (dot(left[0], right[1]) + dot(left[1], right[0]))


def times(value, cos, sin, orient):
    real, imag = value
    if orient < 0:
        return real * cos + imag * sin, imag * cos - real * sin
    return real * cos - imag * sin, imag * cos + real * sin


def add(a, b):
    return a[0] + b[0], a[1] + b[1]


def sub(a, b):
    return a[0] - b[0], a[1] - b[1]


def quarter(a, orient):
    return (a[1], -a[0]) if orient < 0 else (-a[1], a[0])


def constant_turn(value, step, orient):
    step %= 16
    if step == 0:
        return value
    if step == 4:
        return quarter(value, orient)
    angle = 2 * math.pi * step / 16
    return times(value, math.cos(angle), math.sin(angle), orient)


def four(v, orient):
    a, b = add(v[0], v[2]), sub(v[0], v[2])
    c, d = add(v[1], v[3]), quarter(sub(v[1], v[3]), orient)
    return [add(a, c), add(b, d), sub(a, c), sub(b, d)]


def sixteen(v, orient):
    inner = [four([v[n + 4 * m] for m in range(4)], orient) for n in range(4)]
    out = [None] * 16
    for k in range(4):
        for m, value in enumerate(four([constant_turn(inner[n][k], n * k, orient) for n in range(4)], orient)):
            out[k + 4 * m] = value
    return out


def forward_y(values, turn_cos, turn_sin, table):
    spec = sixteen(values, -1)
    spec = [times(spec[k], turn_cos(k), turn_sin(k), -1) for k in range(16)]
    real = jnp.concatenate([s[0] for s in spec], axis=0)
    imag = jnp.concatenate([s[1] for s in spec], axis=0)
    return product(table, split(jnp.concatenate([real, imag], axis=1)), NT)


def inverse_y(block, turn_cos, turn_sin, table):
    spec = product(split(block.T), table, NN)
    spec = [(spec[8 * k : 8 * k + 8, :128], spec[8 * k : 8 * k + 8, 128:]) for k in range(16)]
    return sixteen([times(spec[k], turn_cos(k), turn_sin(k), 1) for k in range(16)], 1)


def forward_x(block, cos, sin, table):
    spec = product(split(block.T), table, NN)
    value = (spec[:, :128].reshape(16, 8, 128), spec[:, 128:].reshape(16, 8, 128))
    parts = times(value, cos[None], sin[None], -1)
    parts = [part.reshape(128, 128) for part in parts]
    return [jnp.concatenate([part[:64], part[64:]], axis=1) for part in parts]


def inverse_x(value, cos, sin, table):
    parts = [jnp.concatenate([p[:, :128], p[:, 128:]], axis=0).reshape(16, 8, 128) for p in (value[:64], value[64:])]
    parts = times(parts, cos[None], sin[None], 1)
    return product(table, split(jnp.concatenate([p.reshape(128, 128) for p in parts], axis=1)), NT)


def kernel(
    fields, radius, coef, muted, small_in, large_in, turns_in, out,
    small, large, turns, mask, vert, vel, ybuf, xsrc, xbuf, ehigh, elow, vsrc, vbuf, wsrc, local, send, recv,
):
    gx, gy = lax.axis_index("gx"), lax.axis_index("gy")
    busy = jnp.logical_or(gx < IDLE_FROM, gx >= IDLE_TO)
    idle = jnp.logical_not(busy)
    barrier = pltpu.get_barrier_semaphore()

    load_vel = pltpu.make_async_copy(fields.at[1], vel, local.at[4])
    load_vel.start()

    def peer_y(k):
        turn = (k - 1) // 2
        far = 4 - (turn + 1) // 2
        y = lax.rem(gy + 8 + jnp.where(lax.rem(turn, 2) == 1, far, -far), 8)
        return 8 * lax.rem(gy // 8 + k, 2) + y

    def peer_x(k):
        turn = k // 4
        far = 4 - (turn + 1) // 2
        z = lax.rem(gx // 4 + 8 + jnp.where(lax.rem(turn, 2) == 1, far, -far), 8)
        return 4 * z + lax.rem(gx + 3 - lax.rem(k, 4), 4)

    def early_x(k):
        return 4 * (k // 4) + lax.rem(gx + k, 4)

    def early_y(k):
        step = k // 2
        y = lax.rem(9 + jnp.where(lax.rem(step, 2) == 1, -((step + 1) // 2), step // 2), 8)
        return 8 * lax.rem(gy // 8 + k, 2) + y

    def greet_y(k, carry):
        pl.semaphore_signal(barrier, inc=1, device_id=(gx, peer_y(k)), device_id_type=MESH)
        return carry

    def greet_x(k, carry):
        pl.semaphore_signal(barrier, inc=1, device_id=(peer_x(k), gy), device_id_type=MESH)
        return carry

    lax.fori_loop(1, GY, greet_y, 0, unroll=True)
    lax.fori_loop(0, GX - 1, greet_x, 0, unroll=True)

    loads = [
        pltpu.make_async_copy(muted.at[0], mask, local.at[0]),
        pltpu.make_async_copy(turns_in, turns, local.at[1]),
        pltpu.make_async_copy(small_in, small, local.at[2]),
        pltpu.make_async_copy(large_in, large, local.at[3]),
    ]
    rows = [pl.ds(8 * c, 8) for c in range(CH)]

    def over_y(phase, c, source, target):
        def one(k, carry):
            peer = peer_y(k + 1) if phase == 0 else early_y(k)

            def go():
                pltpu.make_async_remote_copy(
                src_ref=source(peer), dst_ref=target, send_sem=send.at[phase, c], recv_sem=recv.at[phase, c],
                device_id=(gx, peer), device_id_type=MESH,
                ).start()

            pl.when(peer != gy)(go)
            return carry

        lax.fori_loop(0, GY, one, 0)

    def over_x(phase, c, source, target, busy_only):
        def one(k, carry):
            peer = peer_x(k) if busy_only else early_x(k)

            def go():
                pltpu.make_async_remote_copy(
                    src_ref=source(peer), dst_ref=target, send_sem=send.at[phase, c], recv_sem=recv.at[phase, c],
                    device_id=(peer, gy), device_id_type=MESH,
                ).start()

            if busy_only:
                pl.when(jnp.logical_or(peer < IDLE_FROM, peer >= IDLE_TO))(go)
            else:
                pl.when(peer != gx)(go)
            return carry

        lax.fori_loop(0, GX, one, 0) if not busy_only else lax.fori_loop(0, GX - 1, one, 0)

    def wait(buffer, semaphore):
        pltpu.make_async_copy(buffer, buffer, semaphore).wait()

    def first_y(c):
        over_y(0, c, lambda peer: vel.at[:, peer, rows[c]], ybuf.at[c, gy])

    load_vel.wait()
    pl.semaphore_wait(barrier, GX + GY - 2)
    for c in range(AHEAD):
        first_y(c)
    for load in loads:
        load.start()

    lane = lax.broadcasted_iota(jnp.int32, (16, 128), 1)
    row = lax.broadcasted_iota(jnp.int32, (16, 128), 0)
    ky = 64 * gx + 16 * (lane // 32) + row
    ky_wave = (2.0 * math.pi / NY) * jnp.where(ky < NY // 2, ky, ky - NY).astype(jnp.float32)
    square = radius[0] * radius[0]

    def factor(g, carry):
        columns = pl.ds(pl.multiple_of(128 * g, 128), 128)
        for m in range(4):
            picked = None
            for k in range(4):
                piece = mask[16 * k : 16 * k + 16, columns]
                if k != m:
                    piece = pltpu.roll(piece, 32 * (k - m) % 128, 1)
                picked = piece if picked is None else jnp.where(lane // 32 == k, piece, picked)
            kx = lane % 32 + 32 * (4 * g + m)
            kx_wave = (2.0 * math.pi / NX) * jnp.where(kx < NX // 2, kx, kx - NX).astype(jnp.float32)
            depth = jnp.sqrt(jnp.maximum(square - kx_wave * kx_wave - ky_wave * ky_wave, 0.0))
            depth = depth * (1 - picked).astype(jnp.float32)
            place = pl.ds(pl.multiple_of(32 * g + 8 * m, 8), 8)
            vert[place, 0:128] = depth[0:8]
            vert[place, 128:256] = depth[8:16]
        return carry

    for c in range(CH):
        ybuf[c, gy] = vel[:, gy, rows[c]]
        vbuf[c, IDLE_FROM:IDLE_TO] = jnp.zeros((IDLE_TO - IDLE_FROM, 8, 128), jnp.float32)
    for load in loads:
        load.wait()
    lax.fori_loop(0, 8, factor, 0)

    table_y = (small[0], small[1])
    table_i = (small[2], small[3])

    def turn_y(part):
        return lambda k: turns[16 * part + k : 16 * part + k + 1, :]

    def turn_x(c):
        return turns[pl.ds(32 + 8 * c, 8), :], turns[pl.ds(64 + 8 * c, 8), :]

    for c in range(CH):
        wait(ybuf.at[c, pl.ds(0, GY - 1)], recv.at[0, c])
        if c + AHEAD < CH:
            first_y(c + AHEAD)
        values = [(ybuf[c, j, 0], ybuf[c, j, 1]) for j in range(GY)]
        xsrc[c] = forward_y(values, turn_y(0), turn_y(1), table_y).reshape(GX, 8, 128)
        over_x(1, c, lambda peer: xsrc.at[c, peer], xbuf.at[c, gx], True)
        xbuf[c, gx] = xsrc[c, gx]

    @pl.when(busy)
    def spectrum():
        for c in range(CH):
            wait(xbuf.at[c, pl.ds(0, GX - 1)], recv.at[1, c])
            parts = forward_x(xbuf[c].reshape(256, 128), *turn_x(c), table_i)
            for part in range(2):
                high, low = split(parts[part])
                ehigh[256 * part + 64 * c : 256 * part + 64 * c + 64, :] = high
                elow[256 * part + 64 * c : 256 * part + 64 * c + 64, :] = low

        spec = product((large[0], large[1]), (ehigh[...], elow[...]), NN)
        scale = 0.5 / (NX * NY)
        coef_real, coef_imag = coef[0] * scale, coef[1] * scale
        real, imag = spec[:256], spec[256:]
        depth = vert[...]
        real, imag = (
            depth * coef_real * real - depth * coef_imag * imag,
            depth * coef_real * imag + depth * coef_imag * real,
        )
        high, low = split(jnp.concatenate([real, imag], axis=0))

        for c in range(CH):
            back = (large[2, 128 * c : 128 * c + 128, :], large[3, 128 * c : 128 * c + 128, :])
            value = product(back, (high, low), NN)
            vsrc[c] = inverse_x(value, *turn_x(c), table_i).reshape(GX, 8, 128)
            over_x(2, c, lambda peer: vsrc.at[c, peer], vbuf.at[c, gx], False)
            vbuf[c, gx] = vsrc[c, gx]

    for c in range(CH):
        pl.when(busy)(lambda: wait(vbuf.at[c, pl.ds(0, BUSY - 1)], recv.at[2, c]))
        pl.when(idle)(lambda: wait(vbuf.at[c, pl.ds(0, BUSY)], recv.at[2, c]))
        values = inverse_y(vbuf[c].reshape(256, 128), turn_y(0), turn_y(1), table_y)
        for j in range(GY):
            wsrc[c, j, 0] = values[j][0]
            wsrc[c, j, 1] = values[j][1]
        over_y(3, c, lambda peer: wsrc.at[c, peer], out.at[:, gy, rows[c]])
        pltpu.make_async_copy(wsrc.at[c, gy], out.at[:, gy, rows[c]], local.at[5 + c]).start()

    for c in range(CH):
        wait(ybuf.at[c, pl.ds(0, GY - 1)], send.at[0, c])
        pl.when(busy)(lambda: wait(xbuf.at[c, pl.ds(0, BUSY - 1)], send.at[1, c]))
        pl.when(idle)(lambda: wait(xbuf.at[c, pl.ds(0, BUSY)], send.at[1, c]))
        pl.when(busy)(lambda: wait(vbuf.at[c, pl.ds(0, GX - 1)], send.at[2, c]))
        pltpu.make_async_copy(wsrc.at[c, gy], out.at[:, gy, rows[c]], local.at[5 + c]).wait()
        wait(ybuf.at[c, pl.ds(0, GY - 1)], send.at[3, c])
        wait(ybuf.at[c, pl.ds(0, GY - 1)], recv.at[3, c])


def shards(fields, wavenumber, coupling, evanescent):
    small, large, turns = tables()
    hbm = pl.BlockSpec(memory_space=pltpu.HBM)
    scalars = pl.BlockSpec(memory_space=pltpu.SMEM)
    wave = pl.pallas_call(
        kernel,
        out_shape=pltpu.VMEM((2, GY, 32, 128), jnp.float32),
        in_specs=[hbm, scalars, scalars, hbm, hbm, hbm, hbm],
        out_specs=pl.BlockSpec(memory_space=pl.ANY),
        scratch_shapes=[
            pltpu.VMEM((4, 256, 256), jnp.bfloat16),
            pltpu.VMEM((4, 512, 512), jnp.bfloat16),
            pltpu.VMEM((96, 128), jnp.float32),
            pltpu.VMEM((64, 1024), jnp.int32),
            pltpu.VMEM((256, 256), jnp.float32),
            pltpu.VMEM((2, GY, 32, 128), jnp.float32),
            pltpu.VMEM((CH, GY, 2, 8, 128), jnp.float32),
            pltpu.VMEM((CH, GX, 8, 128), jnp.float32),
            pltpu.VMEM((CH, GX, 8, 128), jnp.float32),
            pltpu.VMEM((512, 256), jnp.bfloat16),
            pltpu.VMEM((512, 256), jnp.bfloat16),
            pltpu.VMEM((CH, GX, 8, 128), jnp.float32),
            pltpu.VMEM((CH, GX, 8, 128), jnp.float32),
            pltpu.VMEM((CH, GY, 2, 8, 128), jnp.float32),
            pltpu.SemaphoreType.DMA((12,)),
            pltpu.SemaphoreType.DMA((4, CH)),
            pltpu.SemaphoreType.DMA((4, CH)),
        ],
        compiler_params=pltpu.CompilerParams(
            collective_id=0, has_side_effects=True, vmem_limit_bytes=60 * 1024 * 1024
        ),
    )(fields, wavenumber, coupling.reshape(2), evanescent, jnp.asarray(small), jnp.asarray(large), jnp.asarray(turns))
    press = 0.5 * fields[0]
    return jnp.stack([press - wave, press + wave])


def solution(mesh):
    in_specs = (P(None, None, None, "gx", "gy"), P("gy"), P(None, "gy"), P("gy", "gx", None))
    out_specs = P(None, None, None, "gx", "gy")
    return jax.shard_map(shards, mesh=mesh, in_specs=in_specs, out_specs=out_specs, check_vma=False)
```

```python
import functools
import math

import jax
import jax.numpy as jnp
import ml_dtypes
import numpy as np
from jax import lax
from jax.experimental import pallas as pl
from jax.experimental.pallas import tpu as pltpu
from jax.sharding import PartitionSpec as P

MESH = pl.DeviceIdType.MESH
NX, NY = 1024, 2048
GX, GY = 32, 16
CH = 4
TOP = int(2.5 * NY / (2 * math.pi))
IDLE_FROM, IDLE_TO = TOP // 64 + 1, (NY - TOP) // 64
BUSY = GX - (IDLE_TO - IDLE_FROM)
NT = (((1,), (1,)), ((), ()))
NN = (((1,), (0,)), ((), ()))


def halves(table):
    high = table.astype(ml_dtypes.bfloat16)
    low = (table - high.astype(np.float64)).astype(ml_dtypes.bfloat16)
    return [high, low]


def real_form(angle):
    cos, sin = np.cos(angle), np.sin(angle)
    return np.array([[cos, sin], [-sin, cos]])


def tables():
    form = real_form(2 * np.pi * (np.arange(128)[:, None] * np.arange(128)[None, :] % 128) / 128)
    wave_y = form.reshape(2, 2, 32, 4, 128).transpose(2, 0, 3, 1, 4).reshape(256, 256)
    form = real_form(2 * np.pi * (np.arange(32)[:, None] * np.arange(32)[None, :] % 32) / 32)
    wave_i = np.einsum("qpim,kl->ipkqlm", form, np.eye(4)).reshape(256, 256)
    wave_r = np.einsum("qpmcr,kl->qmkcplr", form.reshape(2, 2, 32, 4, 8), np.eye(8)).reshape(512, 512)
    small = np.stack(halves(wave_y) + halves(wave_i))
    large = np.stack(halves(wave_r) + halves(wave_r.T))
    turn_y = 2 * np.pi * np.arange(16)[:, None] * np.arange(128)[None, :] / NY
    turn_x = 2 * np.pi * np.arange(32)[:, None] * np.tile(np.arange(32), 4)[None, :] / NX
    turns = np.concatenate([np.cos(turn_y), np.sin(turn_y), np.cos(turn_x), np.sin(turn_x)])
    return small, large, turns.astype(np.float32)


def split(value):
    high = value.astype(jnp.bfloat16)
    low = (value - high.astype(jnp.float32)).astype(jnp.bfloat16)
    return high, low


def product(left, right, dims):
    def dot(a, b):
        return lax.dot_general(a, b, dims, preferred_element_type=jnp.float32)

    return dot(left[0], right[0]) + (dot(left[0], right[1]) + dot(left[1], right[0]))


def times(value, cos, sin, orient):
    real, imag = value
    if orient < 0:
        return real * cos + imag * sin, imag * cos - real * sin
    return real * cos - imag * sin, imag * cos + real * sin


def add(a, b):
    return a[0] + b[0], a[1] + b[1]


def sub(a, b):
    return a[0] - b[0], a[1] - b[1]


def quarter(a, orient):
    return (a[1], -a[0]) if orient < 0 else (-a[1], a[0])


def constant_turn(value, step, orient):
    step %= 16
    if step == 0:
        return value
    if step == 4:
        return quarter(value, orient)
    angle = 2 * math.pi * step / 16
    return times(value, math.cos(angle), math.sin(angle), orient)


def four(v, orient):
    a, b = add(v[0], v[2]), sub(v[0], v[2])
    c, d = add(v[1], v[3]), quarter(sub(v[1], v[3]), orient)
    return [add(a, c), add(b, d), sub(a, c), sub(b, d)]


def sixteen(v, orient):
    inner = [four([v[n + 4 * m] for m in range(4)], orient) for n in range(4)]
    out = [None] * 16
    for k in range(4):
        for m, value in enumerate(four([constant_turn(inner[n][k], n * k, orient) for n in range(4)], orient)):
            out[k + 4 * m] = value
    return out


def forward_y(values, turn_cos, turn_sin, table):
    spec = sixteen(values, -1)
    spec = [times(spec[k], turn_cos(k), turn_sin(k), -1) for k in range(16)]
    real = jnp.concatenate([s[0] for s in spec], axis=0)
    imag = jnp.concatenate([s[1] for s in spec], axis=0)
    return product(table, split(jnp.concatenate([real, imag], axis=1)), NT)


def inverse_y(block, turn_cos, turn_sin, table):
    spec = product(split(block.T), table, NN)
    spec = [(spec[8 * k : 8 * k + 8, :128], spec[8 * k : 8 * k + 8, 128:]) for k in range(16)]
    return sixteen([times(spec[k], turn_cos(k), turn_sin(k), 1) for k in range(16)], 1)


def forward_x(block, cos, sin, table):
    spec = product(split(block.T), table, NN)
    value = (spec[:, :128].reshape(16, 8, 128), spec[:, 128:].reshape(16, 8, 128))
    parts = times(value, cos[None], sin[None], -1)
    parts = [part.reshape(128, 128) for part in parts]
    return [jnp.concatenate([part[:64], part[64:]], axis=1) for part in parts]


def inverse_x(value, cos, sin, table):
    parts = [jnp.concatenate([p[:, :128], p[:, 128:]], axis=0).reshape(16, 8, 128) for p in (value[:64], value[64:])]
    parts = times(parts, cos[None], sin[None], 1)
    return product(table, split(jnp.concatenate([p.reshape(128, 128) for p in parts], axis=1)), NT)


def kernel(
    fields, radius, coef, muted, small_in, large_in, turns_in, out,
    small, large, turns, mask, vert, vel, ybuf, xsrc, xbuf, ehigh, elow, vsrc, vbuf, wsrc, local, send, recv,
):
    gx, gy = lax.axis_index("gx"), lax.axis_index("gy")
    busy = jnp.logical_or(gx < IDLE_FROM, gx >= IDLE_TO)
    idle = jnp.logical_not(busy)
    barrier = pltpu.get_barrier_semaphore()

    load_vel = pltpu.make_async_copy(fields.at[1], vel, local.at[4])
    load_vel.start()

    def peer_y(k):
        turn = (k - 1) // 2
        far = 4 - (turn + 1) // 2
        y = lax.rem(gy + 8 + jnp.where(lax.rem(turn, 2) == 1, far, -far), 8)
        return 8 * lax.rem(gy // 8 + k, 2) + y

    def peer_x(k):
        turn = k // 4
        far = 4 - (turn + 1) // 2
        z = lax.rem(gx // 4 + 8 + jnp.where(lax.rem(turn, 2) == 1, far, -far), 8)
        return 4 * z + lax.rem(gx + 3 - lax.rem(k, 4), 4)

    def early_x(k):
        return 4 * (k // 4) + lax.rem(gx + k, 4)

    def early_y(k):
        step = k // 2
        y = lax.rem(9 + jnp.where(lax.rem(step, 2) == 1, -((step + 1) // 2), step // 2), 8)
        return 8 * lax.rem(gy // 8 + k, 2) + y

    def greet_y(k, carry):
        pl.semaphore_signal(barrier, inc=1, device_id=(gx, peer_y(k)), device_id_type=MESH)
        return carry

    def greet_x(k, carry):
        pl.semaphore_signal(barrier, inc=1, device_id=(peer_x(k), gy), device_id_type=MESH)
        return carry

    lax.fori_loop(1, GY, greet_y, 0, unroll=True)
    lax.fori_loop(0, GX - 1, greet_x, 0, unroll=True)

    loads = [
        pltpu.make_async_copy(muted.at[0], mask, local.at[0]),
        pltpu.make_async_copy(turns_in, turns, local.at[1]),
        pltpu.make_async_copy(small_in, small, local.at[2]),
        pltpu.make_async_copy(large_in, large, local.at[3]),
    ]
    rows = [pl.ds(8 * c, 8) for c in range(CH)]

    def over_y(phase, c, source, target, start=0, stop=GY):
        def one(k, carry):
            peer = peer_y(k + 1) if phase == 0 else early_y(k)

            def go():
                pltpu.make_async_remote_copy(
                    src_ref=source(peer), dst_ref=target, send_sem=send.at[phase, c], recv_sem=recv.at[phase, c],
                    device_id=(gx, peer), device_id_type=MESH,
                ).start()

            pl.when(peer != gy)(go)
            return carry

        lax.fori_loop(start, stop, one, 0, unroll=True)

    def over_x(phase, c, source, target, busy_only, start=0, stop=GX):
        def one(k, carry):
            peer = peer_x(k) if busy_only else early_x(k)

            def go():
                pltpu.make_async_remote_copy(
                    src_ref=source(peer), dst_ref=target, send_sem=send.at[phase, c], recv_sem=recv.at[phase, c],
                    device_id=(peer, gy), device_id_type=MESH,
                ).start()

            if busy_only:
                pl.when(jnp.logical_or(peer < IDLE_FROM, peer >= IDLE_TO))(go)
            else:
                pl.when(peer != gx)(go)
            return carry

        lax.fori_loop(start, stop, one, 0, unroll=True)

    def wait(buffer, semaphore):
        pltpu.make_async_copy(buffer, buffer, semaphore).wait()

    def first_y(c):
        over_y(0, c, lambda peer: vel.at[:, peer, rows[c]], ybuf.at[c, gy])

    load_vel.wait()
    pl.semaphore_wait(barrier, GX + GY - 2)
    for c in range(CH):
        first_y(c)
    for load in loads:
        load.start()

    lane = lax.broadcasted_iota(jnp.int32, (16, 128), 1)
    row = lax.broadcasted_iota(jnp.int32, (16, 128), 0)
    ky = 64 * gx + 16 * (lane // 32) + row
    ky_wave = (2.0 * math.pi / NY) * jnp.where(ky < NY // 2, ky, ky - NY).astype(jnp.float32)
    square = radius[0] * radius[0]

    def factor(g, carry):
        columns = pl.ds(pl.multiple_of(128 * g, 128), 128)
        for m in range(4):
            picked = None
            for k in range(4):
                piece = mask[16 * k : 16 * k + 16, columns]
                if k != m:
                    piece = pltpu.roll(piece, 32 * (k - m) % 128, 1)
                picked = piece if picked is None else jnp.where(lane // 32 == k, piece, picked)
            kx = lane % 32 + 32 * (4 * g + m)
            kx_wave = (2.0 * math.pi / NX) * jnp.where(kx < NX // 2, kx, kx - NX).astype(jnp.float32)
            depth = jnp.sqrt(jnp.maximum(square - kx_wave * kx_wave - ky_wave * ky_wave, 0.0))
            depth = depth * (1 - picked).astype(jnp.float32)
            place = pl.ds(pl.multiple_of(32 * g + 8 * m, 8), 8)
            vert[place, 0:128] = depth[0:8]
            vert[place, 128:256] = depth[8:16]
        return carry

    for c in range(CH):
        ybuf[c, gy] = vel[:, gy, rows[c]]
        vbuf[c, IDLE_FROM:IDLE_TO] = jnp.zeros((IDLE_TO - IDLE_FROM, 8, 128), jnp.float32)
    for load in loads:
        load.wait()
    lax.fori_loop(0, 8, factor, 0)

    table_y = (small[0], small[1])
    table_i = (small[2], small[3])

    def turn_y(part):
        return lambda k: turns[16 * part + k : 16 * part + k + 1, :]

    def turn_x(c):
        return turns[pl.ds(32 + 8 * c, 8), :], turns[pl.ds(64 + 8 * c, 8), :]

    for c in range(CH):
        wait(ybuf.at[c, pl.ds(0, GY - 1)], recv.at[0, c])
        values = [(ybuf[c, j, 0], ybuf[c, j, 1]) for j in range(GY)]
        xsrc[c] = forward_y(values, turn_y(0), turn_y(1), table_y).reshape(GX, 8, 128)
        over_x(1, c, lambda peer: xsrc.at[c, peer], xbuf.at[c, gx], True, 0, GX - 1)
        xbuf[c, gx] = xsrc[c, gx]

    @pl.when(busy)
    def spectrum():
        for c in range(CH):
            wait(xbuf.at[c, pl.ds(0, GX - 1)], recv.at[1, c])
            parts = forward_x(xbuf[c].reshape(256, 128), *turn_x(c), table_i)
            for part in range(2):
                high, low = split(parts[part])
                ehigh[128 * c + 64 * part : 128 * c + 64 * part + 64, :] = high
                elow[128 * c + 64 * part : 128 * c + 64 * part + 64, :] = low
            if c == CH - 2:
                head = product((large[0, :, :384], large[1, :, :384]), (ehigh[:384], elow[:384]), NN)

        spec = head + product((large[0, :, 384:], large[1, :, 384:]), (ehigh[384:], elow[384:]), NN)
        scale = 0.5 / (NX * NY)
        coef_real, coef_imag = coef[0] * scale, coef[1] * scale
        real, imag = spec[:256], spec[256:]
        depth = vert[...]
        real, imag = (
            depth * coef_real * real - depth * coef_imag * imag,
            depth * coef_real * imag + depth * coef_imag * real,
        )
        high, low = split(jnp.concatenate([real, imag], axis=0))

        for c in range(CH):
            back = (large[2, 128 * c : 128 * c + 128, :], large[3, 128 * c : 128 * c + 128, :])
            value = product(back, (high, low), NN)
            vsrc[c] = inverse_x(value, *turn_x(c), table_i).reshape(GX, 8, 128)
            vbuf[c, gx] = vsrc[c, gx]
            over_x(2, c, lambda peer: vsrc.at[c, peer], vbuf.at[c, gx], False)

    for c in range(CH):
        pl.when(busy)(lambda: wait(vbuf.at[c, pl.ds(0, BUSY - 1)], recv.at[2, c]))
        pl.when(idle)(lambda: wait(vbuf.at[c, pl.ds(0, BUSY)], recv.at[2, c]))
        values = inverse_y(vbuf[c].reshape(256, 128), turn_y(0), turn_y(1), table_y)
        for j in range(GY):
            wsrc[c, j, 0] = values[j][0]
            wsrc[c, j, 1] = values[j][1]
        over_y(3, c, lambda peer: wsrc.at[c, peer], out.at[:, gy, rows[c]])
        pltpu.make_async_copy(wsrc.at[c, gy], out.at[:, gy, rows[c]], local.at[5 + c]).start()

    for c in range(CH):
        wait(ybuf.at[c, pl.ds(0, GY - 1)], send.at[0, c])
        pl.when(busy)(lambda: wait(xbuf.at[c, pl.ds(0, BUSY - 1)], send.at[1, c]))
        pl.when(idle)(lambda: wait(xbuf.at[c, pl.ds(0, BUSY)], send.at[1, c]))
        pl.when(busy)(lambda: wait(vbuf.at[c, pl.ds(0, GX - 1)], send.at[2, c]))
        pltpu.make_async_copy(wsrc.at[c, gy], out.at[:, gy, rows[c]], local.at[5 + c]).wait()
        wait(ybuf.at[c, pl.ds(0, GY - 1)], send.at[3, c])
        wait(ybuf.at[c, pl.ds(0, GY - 1)], recv.at[3, c])


def shards(fields, wavenumber, coupling, evanescent):
    small, large, turns = tables()
    hbm = pl.BlockSpec(memory_space=pltpu.HBM)
    scalars = pl.BlockSpec(memory_space=pltpu.SMEM)
    wave = pl.pallas_call(
        kernel,
        out_shape=pltpu.VMEM((2, GY, 32, 128), jnp.float32),
        in_specs=[hbm, scalars, scalars, hbm, hbm, hbm, hbm],
        out_specs=pl.BlockSpec(memory_space=pl.ANY),
        scratch_shapes=[
            pltpu.VMEM((4, 256, 256), jnp.bfloat16),
            pltpu.VMEM((4, 512, 512), jnp.bfloat16),
            pltpu.VMEM((96, 128), jnp.float32),
            pltpu.VMEM((64, 1024), jnp.int32),
            pltpu.VMEM((256, 256), jnp.float32),
            pltpu.VMEM((2, GY, 32, 128), jnp.float32),
            pltpu.VMEM((CH, GY, 2, 8, 128), jnp.float32),
            pltpu.VMEM((CH, GX, 8, 128), jnp.float32),
            pltpu.VMEM((CH, GX, 8, 128), jnp.float32),
            pltpu.VMEM((512, 256), jnp.bfloat16),
            pltpu.VMEM((512, 256), jnp.bfloat16),
            pltpu.VMEM((CH, GX, 8, 128), jnp.float32),
            pltpu.VMEM((CH, GX, 8, 128), jnp.float32),
            pltpu.VMEM((CH, GY, 2, 8, 128), jnp.float32),
            pltpu.SemaphoreType.DMA((12,)),
            pltpu.SemaphoreType.DMA((4, CH)),
            pltpu.SemaphoreType.DMA((4, CH)),
        ],
        compiler_params=pltpu.CompilerParams(
            collective_id=0, has_side_effects=True, vmem_limit_bytes=60 * 1024 * 1024
        ),
    )(fields, wavenumber, coupling.reshape(2), evanescent, jnp.asarray(small), jnp.asarray(large), jnp.asarray(turns))
    press = 0.5 * fields[0]
    return jnp.stack([press - wave, press + wave])


def solution(mesh):
    in_specs = (P(None, None, None, "gx", "gy"), P("gy"), P(None, "gy"), P("gy", "gx", None))
    out_specs = P(None, None, None, "gx", "gy")
    return jax.shard_map(shards, mesh=mesh, in_specs=in_specs, out_specs=out_specs, check_vma=False)
```

```python
import functools
import math

import jax
import jax.numpy as jnp
import ml_dtypes
import numpy as np
from jax import lax
from jax.experimental import pallas as pl
from jax.experimental.pallas import tpu as pltpu
from jax.sharding import PartitionSpec as P

MESH = pl.DeviceIdType.MESH
NX, NY = 1024, 2048
GX, GY = 32, 16
CH = 4
TOP = int(2.5 * NY / (2 * math.pi))
IDLE_FROM, IDLE_TO = TOP // 64 + 1, (NY - TOP) // 64
BUSY = GX - (IDLE_TO - IDLE_FROM)
NT = (((1,), (1,)), ((), ()))
NN = (((1,), (0,)), ((), ()))


def halves(table):
    high = table.astype(ml_dtypes.bfloat16)
    low = (table - high.astype(np.float64)).astype(ml_dtypes.bfloat16)
    return [high, low]


def real_form(angle):
    cos, sin = np.cos(angle), np.sin(angle)
    return np.array([[cos, sin], [-sin, cos]])


def tables():
    form = real_form(2 * np.pi * (np.arange(128)[:, None] * np.arange(128)[None, :] % 128) / 128)
    wave_y = form.reshape(2, 2, 32, 4, 128).transpose(2, 0, 3, 1, 4).reshape(256, 256)
    form = real_form(2 * np.pi * (np.arange(32)[:, None] * np.arange(32)[None, :] % 32) / 32)
    wave_i = np.einsum("qpim,kl->ipkqlm", form, np.eye(4)).reshape(256, 256)
    wave_r = np.einsum("qpmcr,kl->qmkcplr", form.reshape(2, 2, 32, 4, 8), np.eye(8)).reshape(512, 512)
    small = np.stack(halves(wave_y) + halves(wave_i))
    large = np.stack(halves(wave_r) + halves(wave_r.T))
    turn_y = 2 * np.pi * np.arange(16)[:, None] * np.arange(128)[None, :] / NY
    turn_x = 2 * np.pi * np.arange(32)[:, None] * np.tile(np.arange(32), 4)[None, :] / NX
    turns = np.concatenate([np.cos(turn_y), np.sin(turn_y), np.cos(turn_x), np.sin(turn_x)])
    return small, large, turns.astype(np.float32)


def split(value):
    high = value.astype(jnp.bfloat16)
    low = (value - high.astype(jnp.float32)).astype(jnp.bfloat16)
    return high, low


def product(left, right, dims):
    def dot(a, b):
        return lax.dot_general(a, b, dims, preferred_element_type=jnp.float32)

    return dot(left[0], right[0]) + (dot(left[0], right[1]) + dot(left[1], right[0]))


def times(value, cos, sin, orient):
    real, imag = value
    if orient < 0:
        return real * cos + imag * sin, imag * cos - real * sin
    return real * cos - imag * sin, imag * cos + real * sin


def add(a, b):
    return a[0] + b[0], a[1] + b[1]


def sub(a, b):
    return a[0] - b[0], a[1] - b[1]


def quarter(a, orient):
    return (a[1], -a[0]) if orient < 0 else (-a[1], a[0])


def constant_turn(value, step, orient):
    step %= 16
    if step == 0:
        return value
    if step == 4:
        return quarter(value, orient)
    angle = 2 * math.pi * step / 16
    return times(value, math.cos(angle), math.sin(angle), orient)


def four(v, orient):
    a, b = add(v[0], v[2]), sub(v[0], v[2])
    c, d = add(v[1], v[3]), quarter(sub(v[1], v[3]), orient)
    return [add(a, c), add(b, d), sub(a, c), sub(b, d)]


def sixteen(v, orient):
    inner = [four([v[n + 4 * m] for m in range(4)], orient) for n in range(4)]
    out = [None] * 16
    for k in range(4):
        for m, value in enumerate(four([constant_turn(inner[n][k], n * k, orient) for n in range(4)], orient)):
            out[k + 4 * m] = value
    return out


def forward_y(values, turn_cos, turn_sin, table):
    spec = sixteen(values, -1)
    spec = [times(spec[k], turn_cos(k), turn_sin(k), -1) for k in range(16)]
    real = jnp.concatenate([s[0] for s in spec], axis=0)
    imag = jnp.concatenate([s[1] for s in spec], axis=0)
    return product(table, split(jnp.concatenate([real, imag], axis=1)), NT)


def inverse_y(block, turn_cos, turn_sin, table):
    spec = product(split(block.T), table, NN)
    spec = [(spec[8 * k : 8 * k + 8, :128], spec[8 * k : 8 * k + 8, 128:]) for k in range(16)]
    return sixteen([times(spec[k], turn_cos(k), turn_sin(k), 1) for k in range(16)], 1)


def forward_x(block, cos, sin, table):
    spec = product(split(block.T), table, NN)
    value = (spec[:, :128].reshape(16, 8, 128), spec[:, 128:].reshape(16, 8, 128))
    parts = times(value, cos[None], sin[None], -1)
    parts = [part.reshape(128, 128) for part in parts]
    return [jnp.concatenate([part[:64], part[64:]], axis=1) for part in parts]


def inverse_x(value, cos, sin, table):
    parts = [jnp.concatenate([p[:, :128], p[:, 128:]], axis=0).reshape(16, 8, 128) for p in (value[:64], value[64:])]
    parts = times(parts, cos[None], sin[None], 1)
    return product(table, split(jnp.concatenate([p.reshape(128, 128) for p in parts], axis=1)), NT)


def kernel(
    fields, radius, coef, muted, small_in, large_in, turns_in, out,
    small, large, turns, mask, vert, vel, ybuf, xsrc, xbuf, ehigh, elow, vsrc, vbuf, wsrc, local, send, recv,
):
    gx, gy = lax.axis_index("gx"), lax.axis_index("gy")
    busy = jnp.logical_or(gx < IDLE_FROM, gx >= IDLE_TO)
    idle = jnp.logical_not(busy)
    barrier = pltpu.get_barrier_semaphore()

    load_vel = pltpu.make_async_copy(fields.at[1], vel, local.at[4])
    load_vel.start()

    def peer_y(k):
        turn = (k - 1) // 2
        far = 4 - (turn + 1) // 2
        y = lax.rem(gy + 8 + jnp.where(lax.rem(turn, 2) == 1, far, -far), 8)
        return 8 * lax.rem(gy // 8 + k, 2) + y

    def peer_x(k):
        turn = k // 4
        far = 4 - (turn + 1) // 2
        z = lax.rem(gx // 4 + 8 + jnp.where(lax.rem(turn, 2) == 1, far, -far), 8)
        return 4 * z + lax.rem(gx + 3 - lax.rem(k, 4), 4)

    def early_y(k):
        step = k // 2
        y = lax.rem(8 + jnp.where(lax.rem(step, 2) == 1, (step + 1) // 2, -(step // 2)), 8)
        return 8 * lax.rem(k, 2) + y

    def greet_y(k, carry):
        pl.semaphore_signal(barrier, inc=1, device_id=(gx, peer_y(k)), device_id_type=MESH)
        return carry

    def greet_x(k, carry):
        pl.semaphore_signal(barrier, inc=1, device_id=(peer_x(k), gy), device_id_type=MESH)
        return carry

    lax.fori_loop(1, GY, greet_y, 0, unroll=True)
    lax.fori_loop(0, GX - 1, greet_x, 0, unroll=True)

    loads = [
        pltpu.make_async_copy(muted.at[0], mask, local.at[0]),
        pltpu.make_async_copy(turns_in, turns, local.at[1]),
        pltpu.make_async_copy(small_in, small, local.at[2]),
        pltpu.make_async_copy(large_in, large, local.at[3]),
    ]
    rows = [pl.ds(8 * c, 8) for c in range(CH)]

    def over_y(phase, c, source, target, start=0, stop=GY):
        def one(k, carry):
            peer = peer_y(k + 1) if phase == 0 else early_y(k)

            def go():
                pltpu.make_async_remote_copy(
                    src_ref=source(peer), dst_ref=target, send_sem=send.at[phase, c], recv_sem=recv.at[phase, c],
                    device_id=(gx, peer), device_id_type=MESH,
                ).start()

            pl.when(peer != gy)(go)
            return carry

        lax.fori_loop(start, stop, one, 0, unroll=True)

    def over_x(phase, c, source, target, busy_only, start=0, stop=GX):
        def one(k, carry):
            peer = peer_x(k) if busy_only else k

            def go():
                pltpu.make_async_remote_copy(
                    src_ref=source(peer), dst_ref=target, send_sem=send.at[phase, c], recv_sem=recv.at[phase, c],
                    device_id=(peer, gy), device_id_type=MESH,
                ).start()

            if busy_only:
                pl.when(jnp.logical_or(peer < IDLE_FROM, peer >= IDLE_TO))(go)
            else:
                pl.when(peer != gx)(go)
            return carry

        lax.fori_loop(start, stop, one, 0, unroll=True)

    def wait(buffer, semaphore):
        pltpu.make_async_copy(buffer, buffer, semaphore).wait()

    def first_y(c):
        over_y(0, c, lambda peer: vel.at[:, peer, rows[c]], ybuf.at[c, gy])

    load_vel.wait()
    pl.semaphore_wait(barrier, GX + GY - 2)
    for c in range(CH):
        first_y(c)
    for load in loads:
        load.start()

    lane = lax.broadcasted_iota(jnp.int32, (16, 128), 1)
    row = lax.broadcasted_iota(jnp.int32, (16, 128), 0)
    ky = 64 * gx + 16 * (lane // 32) + row
    ky_wave = (2.0 * math.pi / NY) * jnp.where(ky < NY // 2, ky, ky - NY).astype(jnp.float32)
    square = radius[0] * radius[0]

    def factor(g, carry):
        columns = pl.ds(pl.multiple_of(128 * g, 128), 128)
        for m in range(4):
            picked = None
            for k in range(4):
                piece = mask[16 * k : 16 * k + 16, columns]
                if k != m:
                    piece = pltpu.roll(piece, 32 * (k - m) % 128, 1)
                picked = piece if picked is None else jnp.where(lane // 32 == k, piece, picked)
            kx = lane % 32 + 32 * (4 * g + m)
            kx_wave = (2.0 * math.pi / NX) * jnp.where(kx < NX // 2, kx, kx - NX).astype(jnp.float32)
            depth = jnp.sqrt(jnp.maximum(square - kx_wave * kx_wave - ky_wave * ky_wave, 0.0))
            depth = depth * (1 - picked).astype(jnp.float32)
            place = pl.ds(pl.multiple_of(32 * g + 8 * m, 8), 8)
            vert[place, 0:128] = depth[0:8]
            vert[place, 128:256] = depth[8:16]
        return carry

    for c in range(CH):
        ybuf[c, gy] = vel[:, gy, rows[c]]
        vbuf[c, IDLE_FROM:IDLE_TO] = jnp.zeros((IDLE_TO - IDLE_FROM, 8, 128), jnp.float32)
    for load in loads:
        load.wait()
    lax.fori_loop(0, 8, factor, 0)

    table_y = (small[0], small[1])
    table_i = (small[2], small[3])

    def turn_y(part):
        return lambda k: turns[16 * part + k : 16 * part + k + 1, :]

    def turn_x(c):
        return turns[pl.ds(32 + 8 * c, 8), :], turns[pl.ds(64 + 8 * c, 8), :]

    for c in range(CH):
        wait(ybuf.at[c, pl.ds(0, GY - 1)], recv.at[0, c])
        values = [(ybuf[c, j, 0], ybuf[c, j, 1]) for j in range(GY)]
        xsrc[c] = forward_y(values, turn_y(0), turn_y(1), table_y).reshape(GX, 8, 128)
        over_x(1, c, lambda peer: xsrc.at[c, peer], xbuf.at[c, gx], True, 0, GX - 1)
        xbuf[c, gx] = xsrc[c, gx]

    @pl.when(busy)
    def spectrum():
        for c in range(CH):
            wait(xbuf.at[c, pl.ds(0, GX - 1)], recv.at[1, c])
            parts = forward_x(xbuf[c].reshape(256, 128), *turn_x(c), table_i)
            for part in range(2):
                high, low = split(parts[part])
                ehigh[128 * c + 64 * part : 128 * c + 64 * part + 64, :] = high
                elow[128 * c + 64 * part : 128 * c + 64 * part + 64, :] = low
            if c == CH - 2:
                head = product((large[0, :, :384], large[1, :, :384]), (ehigh[:384], elow[:384]), NN)

        spec = head + product((large[0, :, 384:], large[1, :, 384:]), (ehigh[384:], elow[384:]), NN)
        scale = 0.5 / (NX * NY)
        coef_real, coef_imag = coef[0] * scale, coef[1] * scale
        real, imag = spec[:256], spec[256:]
        depth = vert[...]
        real, imag = (
            depth * coef_real * real - depth * coef_imag * imag,
            depth * coef_real * imag + depth * coef_imag * real,
        )
        high, low = split(jnp.concatenate([real, imag], axis=0))

        for c in range(CH):
            back = (large[2, 128 * c : 128 * c + 128, :], large[3, 128 * c : 128 * c + 128, :])
            value = product(back, (high, low), NN)
            vsrc[c] = inverse_x(value, *turn_x(c), table_i).reshape(GX, 8, 128)
            vbuf[c, gx] = vsrc[c, gx]
            over_x(2, c, lambda peer: vsrc.at[c, peer], vbuf.at[c, gx], False)

    for c in range(CH):
        pl.when(busy)(lambda: wait(vbuf.at[c, pl.ds(0, BUSY - 1)], recv.at[2, c]))
        pl.when(idle)(lambda: wait(vbuf.at[c, pl.ds(0, BUSY)], recv.at[2, c]))
        values = inverse_y(vbuf[c].reshape(256, 128), turn_y(0), turn_y(1), table_y)
        for j in range(GY):
            wsrc[c, j, 0] = values[j][0]
            wsrc[c, j, 1] = values[j][1]
        over_y(3, c, lambda peer: wsrc.at[c, peer], out.at[:, gy, rows[c]])
        pltpu.make_async_copy(wsrc.at[c, gy], out.at[:, gy, rows[c]], local.at[5 + c]).start()

    for c in range(CH):
        wait(ybuf.at[c, pl.ds(0, GY - 1)], send.at[0, c])
        pl.when(busy)(lambda: wait(xbuf.at[c, pl.ds(0, BUSY - 1)], send.at[1, c]))
        pl.when(idle)(lambda: wait(xbuf.at[c, pl.ds(0, BUSY)], send.at[1, c]))
        pl.when(busy)(lambda: wait(vbuf.at[c, pl.ds(0, GX - 1)], send.at[2, c]))
        pltpu.make_async_copy(wsrc.at[c, gy], out.at[:, gy, rows[c]], local.at[5 + c]).wait()
        wait(ybuf.at[c, pl.ds(0, GY - 1)], send.at[3, c])
        wait(ybuf.at[c, pl.ds(0, GY - 1)], recv.at[3, c])


def shards(fields, wavenumber, coupling, evanescent):
    small, large, turns = tables()
    hbm = pl.BlockSpec(memory_space=pltpu.HBM)
    scalars = pl.BlockSpec(memory_space=pltpu.SMEM)
    wave = pl.pallas_call(
        kernel,
        out_shape=pltpu.VMEM((2, GY, 32, 128), jnp.float32),
        in_specs=[hbm, scalars, scalars, hbm, hbm, hbm, hbm],
        out_specs=pl.BlockSpec(memory_space=pl.ANY),
        scratch_shapes=[
            pltpu.VMEM((4, 256, 256), jnp.bfloat16),
            pltpu.VMEM((4, 512, 512), jnp.bfloat16),
            pltpu.VMEM((96, 128), jnp.float32),
            pltpu.VMEM((64, 1024), jnp.int32),
            pltpu.VMEM((256, 256), jnp.float32),
            pltpu.VMEM((2, GY, 32, 128), jnp.float32),
            pltpu.VMEM((CH, GY, 2, 8, 128), jnp.float32),
            pltpu.VMEM((CH, GX, 8, 128), jnp.float32),
            pltpu.VMEM((CH, GX, 8, 128), jnp.float32),
            pltpu.VMEM((512, 256), jnp.bfloat16),
            pltpu.VMEM((512, 256), jnp.bfloat16),
            pltpu.VMEM((CH, GX, 8, 128), jnp.float32),
            pltpu.VMEM((CH, GX, 8, 128), jnp.float32),
            pltpu.VMEM((CH, GY, 2, 8, 128), jnp.float32),
            pltpu.SemaphoreType.DMA((12,)),
            pltpu.SemaphoreType.DMA((4, CH)),
            pltpu.SemaphoreType.DMA((4, CH)),
        ],
        compiler_params=pltpu.CompilerParams(
            collective_id=0, has_side_effects=True, vmem_limit_bytes=60 * 1024 * 1024
        ),
    )(fields, wavenumber, coupling.reshape(2), evanescent, jnp.asarray(small), jnp.asarray(large), jnp.asarray(turns))
    press = 0.5 * fields[0]
    return jnp.stack([press - wave, press + wave])


def solution(mesh):
    in_specs = (P(None, None, None, "gx", "gy"), P("gy"), P(None, "gy"), P("gy", "gx", None))
    out_specs = P(None, None, None, "gx", "gy")
    return jax.shard_map(shards, mesh=mesh, in_specs=in_specs, out_specs=out_specs, check_vma=False)
```
